256 devices in a mesh: aux: 4 (over y), bas: 64 (over x, z, core).
Axes of the slice: x: 4, y: 4, z: 8, core: 2. Of those that a mesh axis runs over, the one named last changes fastest.
Arguments:
- integrals: bfloat16 [8, 128, 32, 128, 128], P('aux', 'bas'), may hold values from -6 to 6
- orbitals: bfloat16 [16384, 10240], P('bas'), may hold values from -0.015625 to 0.015625
- screen_list: int32 [128, 32], P('bas'), may hold values from 0 to 127, as said below
- screen_count: int32 [128], P('bas'), may hold values from 16 to 32
- domains: int32 [128, 6], P('bas'), may hold values from 0 to 79, as said below
- pair_list: int32 [128, 4], P('bas'), may hold values from 0 to 127, as said below
Outputs:
- exchange_tiles: bfloat16 [128, 4, 128, 128], P('bas')
The draws below stay inside these ranges and needn't reach their ends.
Inputs may be any that keep to these rules, and one draw needn't show every extreme that they name: `screen_list`: the tiles of one row are distinct; among the 64 entries of the rows of one index of bas, at most 1 name tiles held by any one index of bas, and that many in every draw. `domains`: the 6 entries of a row are distinct. `pair_list`: each entry lies within 2 tiles of its row's own tile.
All inputs are finite; a program needn't handle non-finite values.
Results may differ from the reference program's by a relative error of at most 0.0032.
Values may be sent and summed in bfloat16 or wider, within the bound.
A program may use at most 128 MiB of HBM per device.

```python
import jax
import jax.numpy as jnp
from jax import lax

TILES = 2
TW = 128
DOMB = 6
OCB = 80
KSL = 4
NAUX = 8
NT = 128
SLOTS = 32
NOCC = 10240


def draw_screen_list(key, part):
    key = jax.random.fold_in(key, 11)
    bas_count = NT // TILES
    wanted_count = TILES * SLOTS
    rounds = (wanted_count + bas_count - 1) // bas_count

    def one_device(device):
        subkey = jax.random.fold_in(key, device)
        round_keys = jax.vmap(lambda r: jax.random.fold_in(subkey, r + 2))(jnp.arange(rounds))
        orders = jax.vmap(lambda k: jax.random.permutation(k, bas_count))(round_keys)
        flat = orders.reshape(-1)[:wanted_count]
        rotation = jax.random.randint(jax.random.fold_in(subkey, 1), (), 0, TILES)
        entry = jnp.arange(wanted_count)
        holder = (device + flat) % bas_count
        within = (entry // bas_count + rotation) % TILES
        return (holder * TILES + within).reshape(TILES, SLOTS)
    listed = jax.vmap(one_device)(jnp.arange(bas_count))
    return listed.reshape(NT, SLOTS).astype(jnp.int32)


def draw_domains(key, part):
    key = jax.random.fold_in(key, 12)
    tile_ids = jnp.arange(NT)
    inner = ((tile_ids > 0) & (tile_ids < NT - 1)).astype(jnp.int32)
    jitter = jax.random.randint(jax.random.fold_in(key, 1), (NT,), 0, 2) * inner
    rotation = jax.random.randint(jax.random.fold_in(key, 2), (NT,), 0, DOMB)
    base = tile_ids * (OCB - DOMB) // max(NT - 1, 1)
    base = jnp.minimum(base + jitter, OCB - DOMB)
    slot_ids = jnp.arange(DOMB)
    turned = (slot_ids[None, :] + rotation[:, None]) % DOMB
    return (base[:, None] + turned).astype(jnp.int32)


def draw_pair_list(key, part):
    key = jax.random.fold_in(key, 13)
    offsets = jax.random.randint(key, (NT, KSL), -TILES, TILES + 1)
    tile_ids = jnp.arange(NT)
    return jnp.clip(tile_ids[:, None] + offsets, 0, NT - 1).astype(jnp.int32)


def place_ends(result, rng, low, top_value):
    place = [jax.random.randint(jax.random.fold_in(rng, axis), (), 0, length) for axis, length in enumerate(result.shape)]
    widest = result.shape.index(max(result.shape))
    beside = place[:widest] + [(place[widest] + 1) % result.shape[widest]] + place[widest + 1:]
    return result.at[tuple(place)].set(low).at[tuple(beside)].set(top_value)


def levels(key, shape, shards, low, high):
    gain, own = 1.0, jax.random.fold_in(key, 6)
    for position, shards_of in shards:
        heights = jnp.exp(jax.random.uniform(jax.random.fold_in(own, position), (shards_of,), jnp.float32, low / len(shards), high / len(shards)))
        gain = gain * jnp.repeat(heights, shape[position] // shards_of).reshape([-1 if axis == position else 1 for axis in range(len(shape))])
    return gain


def scatter_about(rng, extent, spread, most, shards=(), dtype=jnp.bfloat16):
    level = levels(rng, extent, shards, -0.22, 0.18) if shards else 1.0
    drawn = jax.random.normal(rng, extent, jnp.float32) * spread * level
    return jnp.minimum(jnp.maximum(drawn, -most), most).astype(dtype)


def setup_inputs(seed: int = 0) -> dict:
    splits = jax.random.split(jax.random.key(seed), 7)
    integrals = scatter_about(splits[0], (NAUX, NT, SLOTS, TW, TW), 1.0, 6.0, ((0, 4), (1, 64)))
    orbitals = scatter_about(splits[1], (NT * TW, NOCC), (SLOTS * 4096) ** -0.5, 0.015625, ((0, 64),))
    screen_list = draw_screen_list(jax.random.fold_in(splits[6], 71), 0)
    screen_count = place_ends(jax.random.randint(splits[3], (NT,), SLOTS // 2, SLOTS + 1), jax.random.fold_in(splits[3], 1), SLOTS // 2, SLOTS).astype(jnp.int32)
    domains = draw_domains(jax.random.fold_in(splits[6], 71), 0)
    pair_list = draw_pair_list(jax.random.fold_in(splits[6], 71), 0)
    return dict(integrals=integrals, orbitals=orbitals, screen_list=screen_list, screen_count=screen_count, domains=domains, pair_list=pair_list)


def reference(integrals, orbitals, screen_list, screen_count, domains, pair_list):
    blocked = orbitals.reshape(NT, TW, OCB, TW)

    def half_tile(tile):
        slab = lax.dynamic_index_in_dim(integrals, tile, 1, keepdims=False)
        picked = blocked[screen_list[tile][:, None], :, domains[tile][None, :], :]
        active = (jnp.arange(SLOTS) < screen_count[tile]).astype(jnp.float32)
        picked = picked.astype(jnp.float32) * active[:, None, None, None]
        return jnp.einsum("psab,sdbo->apdo", slab.astype(jnp.float32), picked).astype(jnp.bfloat16)

    halfway = lax.map(half_tile, jnp.arange(NT))

    def pair_tile(tile):
        partners = pair_list[tile]
        partner_half = halfway[partners].astype(jnp.float32)
        partner_dom = domains[partners]
        intersection = (domains[tile][None, :, None] == partner_dom[:, None, :]).astype(jnp.float32)
        aligned = jnp.einsum("kde,kbpeo->kbpdo", intersection, partner_half).astype(jnp.bfloat16)
        own_half = halfway[tile].astype(jnp.float32)
        summed = jnp.einsum("apdo,kbpdo->kab", own_half, aligned.astype(jnp.float32))
        return summed.astype(jnp.bfloat16)

    return lax.map(pair_tile, jnp.arange(NT))
```

```python
import functools

import jax
import jax.numpy as jnp
from jax import lax
from jax.experimental import pallas as pl
from jax.experimental.pallas import tpu as pltpu
from jax.sharding import PartitionSpec as P

MESH = pl.DeviceIdType.MESH
TW = 128
DOM = 6
DIRECT = 16
HALF = 2 * DIRECT
ROWS = 4 * TW
LANE_TILE, LANE_DOM, LANE_SLOT, LANE_ROW, LANE_ON = 0, 1, 7, 8, 9


def kernel(
    lists_ref, count_ref, dom_ref, pair_ref, integrals_ref, orbitals_ref, out_ref,
    ints, orbs, rec, rec_s, req, req_s, domv, dom_s, match_s,
    sent, rhs, ints_out, ints_in, lhs, own, other, other_in, halo, tiles, tiles_in, result,
    load_sem, rec_send, rec_recv, dom_send, dom_recv,
    block_send, block_recv, pass_send, pass_recv, ints_sem,
    part_send, part_recv, halo_send, halo_recv, tile_send, tile_recv, res_send, res_recv,
):
    y, bas = lax.axis_index("aux"), lax.axis_index("bas")
    x, z, c = bas // 16, (bas // 2) % 8, bas % 2
    y0, y1 = y % 2, y // 2
    partner, mate = y + 1 - 2 * y0, 3 - y
    before, after = (bas + 63) % 64, (bas + 1) % 64

    def place(px, pz, pc):
        return (((px + 8) % 4) * 8 + (pz + 16) % 8) * 2 + pc

    def target(i):
        return place(x - i // 4, z - 2 * (i % 4) - (c + y0) % 2, (y0 + y1 + c) % 2)

    def holder(plane0, plane1, i):
        return place(x + i // 4, z + 2 * (i % 4) + (c + plane1) % 2, (plane0 + plane1 + c) % 2)

    def half_holder(plane0, j):
        q = j // DIRECT
        return holder((plane0 + q) % 2, (y1 + q) % 2, j % DIRECT)

    load_ints = pltpu.make_async_copy(integrals_ref, ints, load_sem.at[0])
    load_orbs = pltpu.make_async_copy(orbitals_ref, orbs, load_sem.at[1])
    load_ints.start()
    load_orbs.start()

    barrier = pltpu.get_barrier_semaphore()

    def greet(device):
        pl.semaphore_signal(barrier, inc=1, device_id=device, device_id_type=MESH)

    @pl.loop(0, DIRECT)
    def _(i):
        @pl.when(target(i) != bas)
        def _():
            greet({"bas": target(i)})

        @pl.when(holder(y0, y1, i) != bas)
        def _():
            greet({"bas": holder(y0, y1, i)})

    for r in range(1, 4):
        greet({"aux": (y + r) % 4})
    greet({"bas": before})
    greet({"bas": after})

    holder_ids = lax.broadcasted_iota(jnp.int32, (64, 32), 0)
    slot_ids = lax.broadcasted_iota(jnp.int32, (64, 32), 1)
    lanes = lax.broadcasted_iota(jnp.int32, (64, TW), 1)
    table = jnp.zeros((64, TW), jnp.int32)
    for m in range(2):
        row = lists_ref[m : m + 1, :]
        hit = (row >> 1) == holder_ids
        found = jnp.sum(jnp.where(hit, 1, 0), axis=1, keepdims=True)
        tile = jnp.sum(jnp.where(hit, row & 1, 0), axis=1, keepdims=True)
        slot = jnp.sum(jnp.where(hit, slot_ids, 0), axis=1, keepdims=True)
        on = found * jnp.where(slot < count_ref[m], 1, 0)
        table += jnp.where(lanes == LANE_TILE, tile, 0)
        table += jnp.where(lanes == LANE_SLOT, slot + found * (32 * m), 0)
        table += jnp.where(lanes == LANE_ROW, found * m, 0)
        table += jnp.where(lanes == LANE_ON, on, 0)
        for d in range(DOM):
            table += jnp.where(lanes == LANE_DOM + d, found * dom_ref[m, d], 0)
    rec[...] = jnp.clip(table, 0, 79)
    lane = lax.broadcasted_iota(jnp.int32, (8, TW), 1)
    mine = jnp.zeros((8, TW), jnp.int32)
    for m in range(2):
        for d in range(DOM):
            mine += jnp.where(lane == m * DOM + d, dom_ref[m, d], 0)
    domv[1] = mine
    rec_local = pltpu.make_async_copy(rec, rec_s, load_sem.at[2])
    rec_local.start()

    alone = ((y0 + y1 + 1) % 2) * ((c + y0 + 1) % 2)
    pl.semaphore_wait(barrier, 2 * DIRECT + 5 - 2 * alone)

    def rec_copy(i):
        return pltpu.make_async_remote_copy(
            src_ref=rec.at[pl.ds(holder(y0, y1, i), 1), :], dst_ref=req.at[pl.ds(i, 1), :],
            send_sem=rec_send.at[i], recv_sem=rec_recv.at[i],
            device_id={"bas": holder(y0, y1, i)}, device_id_type=MESH,
        )

    def rec_self(i):
        return pltpu.make_async_copy(
            rec.at[pl.ds(holder(y0, y1, i), 1), :], req.at[pl.ds(i, 1), :], rec_recv.at[i]
        )

    @pl.loop(0, DIRECT)
    def _(i):
        @pl.when(holder(y0, y1, i) != bas)
        def _():
            rec_copy(i).start()

        @pl.when(holder(y0, y1, i) == bas)
        def _():
            rec_self(i).start()

    def dom_copy(way):
        return pltpu.make_async_remote_copy(
            src_ref=domv.at[1], dst_ref=domv.at[2 - 2 * way],
            send_sem=dom_send.at[way], recv_sem=dom_recv.at[way],
            device_id={"bas": after if way else before}, device_id_type=MESH,
        )

    dom_copy(0).start()
    dom_copy(1).start()

    def slot_of(at):
        return jnp.minimum(rec_s[at, LANE_SLOT], 63)

    rec_local.wait()
    load_ints.wait()

    @pl.loop(0, HALF)
    def _(j):
        slot = slot_of(half_holder((y0 + 1) % 2, j))
        for p in range(2):
            ints_out[j, p] = ints[p, slot]

    ints_copy = pltpu.make_async_remote_copy(
        src_ref=ints_out, dst_ref=ints_in, send_sem=ints_sem.at[0], recv_sem=ints_sem.at[1],
        device_id={"aux": partner}, device_id_type=MESH,
    )
    ints_copy.start()

    @pl.loop(0, DIRECT)
    def _(i):
        rec_self(i).wait()

    req_local = pltpu.make_async_copy(req, req_s, load_sem.at[3])
    req_local.start()
    req_local.wait()
    load_orbs.wait()

    def rows_of(i):
        return pl.ds(pl.multiple_of(i * TW, TW), TW)

    def block_copy(g, i):
        return pltpu.make_async_remote_copy(
            src_ref=sent.at[g, i], dst_ref=rhs.at[g, rows_of(i), :],
            send_sem=block_send.at[g, i], recv_sem=block_recv.at[g, i],
            device_id={"bas": target(i)}, device_id_type=MESH,
        )

    def block_self(g, i):
        return pltpu.make_async_copy(sent.at[g, i], rhs.at[g, rows_of(i), :], block_recv.at[g, i])

    def pass_copy(g, i):
        return pltpu.make_async_remote_copy(
            src_ref=rhs.at[g, rows_of(i), :], dst_ref=rhs.at[g, rows_of(DIRECT + i), :],
            send_sem=pass_send.at[g], recv_sem=pass_recv.at[g],
            device_id={"aux": mate}, device_id_type=MESH,
        )

    @pl.loop(0, DOM * DIRECT)
    def _(t):
        g, i = t // DIRECT, t % DIRECT
        top = jnp.minimum(req_s[i, LANE_TILE], 1) * TW
        left = req_s[i, LANE_DOM + g] * TW
        sent[g, i] = orbs[pl.ds(top, TW), pl.ds(left, TW)]

        @pl.when(target(i) != bas)
        def _():
            block_copy(g, i).start()

        @pl.when(target(i) == bas)
        def _():
            block_self(g, i).start()

    def fill(j, base, read):
        at = half_holder(y0, j)
        cols = pl.ds(pl.multiple_of(j * TW, TW), TW)
        for m in range(2):
            keep = rec_s[at, LANE_ON] * jnp.where(rec_s[at, LANE_ROW] == m, 1, 0)
            scale = keep.astype(jnp.float32)
            for p in range(2):
                part = read(at, p).astype(jnp.float32) * scale
                lhs[pl.ds(base + (2 * m + p) * TW, TW), cols] = part.astype(jnp.bfloat16)

    @pl.loop(0, HALF)
    def _(j):
        fill(j, 0, lambda at, p: ints[p, slot_of(at)])

    rec_doms = [dom_copy(0), dom_copy(1)]
    for copy in rec_doms:
        copy.wait()
    dom_local = pltpu.make_async_copy(domv, dom_s, load_sem.at[4])
    dom_local.start()
    dom_local.wait()

    @pl.loop(0, 8)
    def _(t):
        m, k = t // 4, t % 4
        n = jnp.clip(pair_ref[m, k] - 2 * bas + 2, 0, 5)
        side, row = n >> 1, n & 1
        match_s[t, 12] = side
        match_s[t, 13] = row
        for d in range(DOM):
            at, some = 0, 0
            for e in range(DOM):
                same = jnp.where(dom_s[side, 0, row * DOM + e] == dom_ref[m, d], 1, 0)
                at, some = at + same * e, some + same
            match_s[t, d] = jnp.minimum(at, DOM - 1)
            match_s[t, DOM + d] = some

    def whole(ref, sem):
        return pltpu.make_async_copy(ref, ref, sem)

    def part_copy(g):
        return pltpu.make_async_remote_copy(
            src_ref=other.at[g], dst_ref=other_in.at[g],
            send_sem=part_send.at[g], recv_sem=part_recv.at[g],
            device_id={"aux": partner}, device_id_type=MESH,
        )

    def halo_copy(g, way):
        return pltpu.make_async_remote_copy(
            src_ref=halo.at[1, g], dst_ref=halo.at[2 - 2 * way, g],
            send_sem=halo_send.at[g, way], recv_sem=halo_recv.at[g, way],
            device_id={"bas": after if way else before}, device_id_type=MESH,
        )

    def contract(into, base, g):
        into[g] = jnp.dot(lhs[base : base + ROWS, :], rhs[g], preferred_element_type=jnp.float32)

    def finish(g):
        part_copy(g).wait_recv()
        for m in range(2):
            for p in range(2):
                rows = pl.ds((2 * m + p) * TW, TW)
                total = own[g, rows, :] + other_in[g, rows, :]
                halo[1, g, m, :, p * TW : (p + 1) * TW] = total.astype(jnp.bfloat16)
        halo_copy(g, 0).start()
        halo_copy(g, 1).start()

    def passed(g):
        whole(rhs.at[g, pl.ds(DIRECT * TW, DIRECT * TW), :], pass_recv.at[g]).wait()

    for g in range(DOM):
        @pl.loop(0, DIRECT)
        def _(i):
            block_self(g, i).wait()
            pass_copy(g, i).start()

        if g == 4:
            ints_copy.wait_recv()

            @pl.loop(0, HALF)
            def _(j):
                fill(j, ROWS, lambda at, p: ints_in[j, p])

            for early in range(3):
                contract(other, ROWS, early)
                part_copy(early).start()
        if g >= 1:
            passed(g - 1)
            if g >= 4:
                contract(other, ROWS, g - 1)
                part_copy(g - 1).start()
            contract(own, 0, g - 1)
    last = DOM - 1
    for g in range(last - 1):
        finish(g)
    passed(last)
    contract(other, ROWS, last)
    part_copy(last).start()
    contract(own, 0, last)
    finish(last - 1)
    finish(last)
    for g in range(DOM):
        halo_copy(g, 0).wait_recv()
        halo_copy(g, 1).wait_recv()

    def tile_copy(r):
        owner = (y + r) % 4
        return pltpu.make_async_remote_copy(
            src_ref=tiles.at[pl.ds(2 * owner, 2)], dst_ref=tiles_in.at[r - 1],
            send_sem=tile_send.at[r - 1], recv_sem=tile_recv.at[r - 1],
            device_id={"aux": owner}, device_id_type=MESH,
        )

    def res_copy(r):
        return pltpu.make_async_remote_copy(
            src_ref=result.at[pl.ds(2 * y, 2)], dst_ref=result.at[pl.ds(2 * y, 2)],
            send_sem=res_send.at[r - 1], recv_sem=res_recv.at[r - 1],
            device_id={"aux": (y + r) % 4}, device_id_type=MESH,
        )

    for r in (2, 1, 3, 0):
        @pl.loop(0, 2)
        def _(s):
            t = 2 * ((y + r) % 4) + s
            side, row = match_s[t, 12], match_s[t, 13]
            total = jnp.zeros((TW, TW), jnp.float32)
            for d in range(DOM):
                there = halo[side, match_s[t, d], row]
                scale = match_s[t, DOM + d].astype(jnp.float32)
                here = halo[1, d, t // 4]
                part = lax.dot_general(
                    here, there, (((1,), (1,)), ((), ())), preferred_element_type=jnp.float32
                )
                total += part * scale
            tiles[t] = total

        if r:
            tile_copy(r).start()
    for r in range(1, 4):
        tile_copy(r).wait_recv()
    total = tiles[pl.ds(2 * y, 2)] + tiles_in[0] + tiles_in[1] + tiles_in[2]
    result[pl.ds(2 * y, 2)] = total.astype(jnp.bfloat16)
    for r in (2, 1, 3):
        res_copy(r).start()

    @pl.loop(0, DOM * DIRECT)
    def _(t):
        g, i = t // DIRECT, t % DIRECT

        @pl.when(target(i) != bas)
        def _():
            block_copy(g, i).wait_send()

    @pl.loop(0, DIRECT)
    def _(i):
        @pl.when(holder(y0, y1, i) != bas)
        def _():
            rec_copy(i).wait_send()

    for g in range(DOM):
        whole(rhs.at[g, pl.ds(0, DIRECT * TW), :], pass_send.at[g]).wait()
        part_copy(g).wait_send()
        halo_copy(g, 0).wait_send()
        halo_copy(g, 1).wait_send()
    ints_copy.wait_send()
    for r in range(1, 4):
        tile_copy(r).wait_send()
        res_copy(r).wait()
    out_ref[...] = result[...]


def on_device(integrals, orbitals, screen_list, screen_count, domains, pair_list):
    vmem, smem = pl.BlockSpec(memory_space=pltpu.VMEM), pl.BlockSpec(memory_space=pltpu.SMEM)
    hbm = pl.BlockSpec(memory_space=pl.ANY)
    dma, bf16, f32, i32 = pltpu.SemaphoreType.DMA, jnp.bfloat16, jnp.float32, jnp.int32
    out = pl.pallas_call(
        kernel,
        out_shape=jax.ShapeDtypeStruct((8, TW, TW), bf16),
        in_specs=[vmem, smem, smem, smem, hbm, hbm],
        out_specs=vmem,
        scratch_shapes=[
            pltpu.VMEM((2, 64, TW, TW), bf16),
            pltpu.VMEM(orbitals.shape, bf16),
            pltpu.VMEM((64, TW), i32),
            pltpu.SMEM((64, TW), i32),
            pltpu.VMEM((DIRECT, TW), i32),
            pltpu.SMEM((DIRECT, TW), i32),
            pltpu.VMEM((3, 8, TW), i32),
            pltpu.SMEM((3, 8, TW), i32),
            pltpu.SMEM((8, 16), i32),
            pltpu.VMEM((DOM, DIRECT, TW, TW), bf16),
            pltpu.VMEM((DOM, HALF * TW, TW), bf16),
            pltpu.VMEM((HALF, 2, TW, TW), bf16),
            pltpu.VMEM((HALF, 2, TW, TW), bf16),
            pltpu.VMEM((2 * ROWS, HALF * TW), bf16),
            pltpu.VMEM((DOM, ROWS, TW), f32),
            pltpu.VMEM((DOM, ROWS, TW), f32),
            pltpu.VMEM((DOM, ROWS, TW), f32),
            pltpu.VMEM((3, DOM, 2, TW, 2 * TW), bf16),
            pltpu.VMEM((8, TW, TW), f32),
            pltpu.VMEM((3, 2, TW, TW), f32),
            pltpu.VMEM((8, TW, TW), bf16),
            dma((5,)), dma((DIRECT,)), dma((DIRECT,)), dma((2,)), dma((2,)),
            dma((DOM, DIRECT)), dma((DOM, DIRECT)), dma((DOM,)), dma((DOM,)), dma((2,)),
            dma((DOM,)), dma((DOM,)), dma((DOM, 2)), dma((DOM, 2)), dma((3,)), dma((3,)), dma((3,)), dma((3,)),
        ],
        compiler_params=pltpu.CompilerParams(
            collective_id=0, has_side_effects=True, vmem_limit_bytes=52 * 2**20
        ),
    )(
        screen_list, screen_count, domains, pair_list,
        integrals.reshape(2, 64, TW, TW), orbitals,
    )
    return out.reshape(2, 4, TW, TW)


def solution(mesh):
    in_specs = (
        P("aux", "bas", None, None, None),
        P("bas", None),
        P("bas", None),
        P("bas"),
        P("bas", None),
        P("bas", None),
    )
    return jax.shard_map(
        on_device, mesh=mesh, in_specs=in_specs, out_specs=P("bas", None, None, None), check_vma=False
    )
```

```python
import functools

import jax
import jax.numpy as jnp
from jax import lax
from jax.experimental import pallas as pl
from jax.experimental.pallas import tpu as pltpu
from jax.sharding import PartitionSpec as P

MESH = pl.DeviceIdType.MESH
TW = 128
DOM = 6
FAR = 14
NEAR = 8
HALF = 2 * FAR
HELD = HALF + NEAR
ROWS = 4 * TW
LANE_TILE, LANE_DOM, LANE_SLOT, LANE_ROW, LANE_ON = 0, 1, 7, 8, 9


def kernel(
    lists_ref, count_ref, dom_ref, pair_ref, integrals_ref, orbitals_ref, out_ref,
    lists, count, dom, pair,
    ints, orbs, rec, rec_s, req, req_s, domv, dom_s, match_s,
    sent, rhs, ints_out, ints_in, lhs, own, other, other_in, halo, tiles, tiles_in, result,
    load_sem, rec_send, rec_recv, dom_send, dom_recv,
    block_send, block_recv, pass_send, pass_recv, ints_sem,
    part_send, part_recv, halo_send, halo_recv, tile_send, tile_recv, res_send, res_recv,
):
    y, bas = lax.axis_index("aux"), lax.axis_index("bas")
    x, z, c = lax.div(bas, 16), lax.rem(lax.div(bas, 2), 8), lax.rem(bas, 2)
    y0, y1 = lax.rem(y, 2), lax.div(y, 2)
    partner, mate = y + 1 - 2 * y0, 3 - y
    before, after = lax.rem(bas + 63, 64), lax.rem(bas + 1, 64)

    def place(px, pz, pc):
        return lax.rem(px, 4) * 16 + lax.rem(pz, 8) * 2 + pc

    def offset(parity, i):
        dz = lax.rem(i, 7) + 1
        return 2 * lax.div(i, 7) + lax.rem(dz + parity, 2), dz

    out_parity = lax.rem(c + y0, 2)
    out_core = lax.rem(y0 + y1 + c, 2)

    def target(i):
        dx, dz = offset(out_parity, i)
        return place(x + 4 - dx, z + 8 - dz, out_core)

    def holder(plane0, plane1, i):
        dx, dz = offset(lax.rem(c + plane1, 2), i)
        return place(x + dx, z + dz, lax.rem(plane0 + plane1 + c, 2))

    def half_holder(plane0, j):
        q = lax.div(j, FAR)
        return holder(lax.rem(plane0 + q, 2), lax.rem(y1 + q, 2), lax.rem(j, FAR))

    def near_target(v):
        return place(x + 4 - lax.div(v, 2), z, lax.rem(c + v, 2))

    def near_holder(v):
        return place(x + lax.div(v, 2), z, lax.rem(c + v, 2))

    small = [
        pltpu.make_async_copy(a, b, load_sem.at[5 + i])
        for i, (a, b) in enumerate(
            [(lists_ref, lists), (count_ref, count), (dom_ref, dom), (pair_ref, pair)]
        )
    ]
    load_ints = pltpu.make_async_copy(integrals_ref, ints, load_sem.at[0])
    load_orbs = pltpu.make_async_copy(orbitals_ref, orbs, load_sem.at[1])
    for copy in small:
        copy.start()
    load_ints.start()
    load_orbs.start()

    barrier = pltpu.get_barrier_semaphore()

    def greet(device):
        pl.semaphore_signal(barrier, inc=1, device_id=device, device_id_type=MESH)

    @pl.loop(0, FAR)
    def _(i):
        greet({"bas": target(i)})
        greet({"bas": holder(y0, y1, i)})

    @pl.loop(1, NEAR)
    def _(v):
        greet({"bas": near_target(v)})

    for r in range(1, 4):
        greet({"aux": lax.rem(y + r, 4)})
    greet({"bas": before})
    greet({"bas": after})

    for copy in small:
        copy.wait()

    holder_ids = lax.broadcasted_iota(jnp.int32, (64, 32), 0)
    slot_ids = lax.broadcasted_iota(jnp.int32, (64, 32), 1)
    lanes = lax.broadcasted_iota(jnp.int32, (64, TW), 1)
    table = jnp.zeros((64, TW), jnp.int32)
    for m in range(2):
        row = lists[m : m + 1, :]
        hit = (row >> 1) == holder_ids
        found = jnp.sum(jnp.where(hit, 1, 0), axis=1, keepdims=True)
        tile = jnp.sum(jnp.where(hit, row & 1, 0), axis=1, keepdims=True)
        slot = jnp.sum(jnp.where(hit, slot_ids, 0), axis=1, keepdims=True)
        on = found * jnp.where(slot < count[m], 1, 0)
        table += jnp.where(lanes == LANE_TILE, tile, 0)
        table += jnp.where(lanes == LANE_SLOT, slot + found * (32 * m), 0)
        table += jnp.where(lanes == LANE_ROW, found * m, 0)
        table += jnp.where(lanes == LANE_ON, on, 0)
        for d in range(DOM):
            table += jnp.where(lanes == LANE_DOM + d, found * dom[m, d], 0)
    rec[...] = jnp.clip(table, 0, 79)
    lane = lax.broadcasted_iota(jnp.int32, (8, TW), 1)
    mine = jnp.zeros((8, TW), jnp.int32)
    for m in range(2):
        for d in range(DOM):
            mine += jnp.where(lane == m * DOM + d, dom[m, d], 0)
    domv[1] = mine
    rec_local = pltpu.make_async_copy(rec, rec_s, load_sem.at[2])
    rec_local.start()

    pl.semaphore_wait(barrier, 2 * FAR + NEAR - 1 + 5)

    def rec_copy(i, device):
        return pltpu.make_async_remote_copy(
            src_ref=rec.at[pl.ds(device, 1), :], dst_ref=req.at[pl.ds(i, 1), :],
            send_sem=rec_send.at[i], recv_sem=rec_recv.at[i],
            device_id={"bas": device}, device_id_type=MESH,
        )

    def rec_far(i):
        return rec_copy(i, holder(y0, y1, i))

    def rec_near(v):
        return rec_copy(FAR + v, near_holder(v))

    rec_self = pltpu.make_async_copy(rec.at[pl.ds(bas, 1), :], req.at[pl.ds(FAR, 1), :], rec_recv.at[FAR])

    @pl.loop(0, FAR)
    def _(i):
        rec_far(i).start()

    @pl.loop(1, NEAR)
    def _(v):
        rec_near(v).start()

    rec_self.start()

    def dom_copy(way):
        return pltpu.make_async_remote_copy(
            src_ref=domv.at[1], dst_ref=domv.at[2 - 2 * way],
            send_sem=dom_send.at[way], recv_sem=dom_recv.at[way],
            device_id={"bas": after if way else before}, device_id_type=MESH,
        )

    dom_copy(0).start()
    dom_copy(1).start()

    def slot_of(at):
        return jnp.minimum(rec_s[at, LANE_SLOT], 63)

    rec_local.wait()
    load_ints.wait()

    @pl.loop(0, HALF)
    def _(j):
        slot = slot_of(half_holder(lax.rem(y0 + 1, 2), j))
        for p in range(2):
            ints_out[j, p] = ints[p, slot]

    ints_copy = pltpu.make_async_remote_copy(
        src_ref=ints_out, dst_ref=ints_in, send_sem=ints_sem.at[0], recv_sem=ints_sem.at[1],
        device_id={"aux": partner}, device_id_type=MESH,
    )
    ints_copy.start()

    rec_self.wait()

    @pl.loop(0, FAR)
    def _(i):
        rec_far(i).wait_recv()

    @pl.loop(1, NEAR)
    def _(v):
        rec_near(v).wait_recv()

    req_local = pltpu.make_async_copy(req, req_s, load_sem.at[3])
    req_local.start()
    req_local.wait()
    load_orbs.wait()

    def rows_of(i):
        return pl.ds(pl.multiple_of(i * TW, TW), TW)

    def block_copy(g, i):
        return pltpu.make_async_remote_copy(
            src_ref=sent.at[g, i], dst_ref=rhs.at[g, rows_of(i), :],
            send_sem=block_send.at[g, i], recv_sem=block_recv.at[g, i],
            device_id={"bas": target(i)}, device_id_type=MESH,
        )

    def near_copy(g, v):
        return pltpu.make_async_remote_copy(
            src_ref=sent.at[g, FAR + v], dst_ref=rhs.at[g, rows_of(HALF + v), :],
            send_sem=block_send.at[g, FAR + v], recv_sem=block_recv.at[g, FAR + v],
            device_id={"bas": near_target(v)}, device_id_type=MESH,
        )

    def self_copy(g):
        return pltpu.make_async_copy(
            sent.at[g, FAR], rhs.at[g, pl.ds(HALF * TW, TW), :], block_recv.at[g, FAR]
        )

    def pass_copy(g, i):
        return pltpu.make_async_remote_copy(
            src_ref=rhs.at[g, rows_of(i), :], dst_ref=rhs.at[g, rows_of(FAR + i), :],
            send_sem=pass_send.at[g], recv_sem=pass_recv.at[g],
            device_id={"aux": mate}, device_id_type=MESH,
        )

    def pick(g, i):
        top = jnp.minimum(req_s[i, LANE_TILE], 1) * TW
        left = req_s[i, LANE_DOM + g] * TW
        sent[g, i] = orbs[pl.ds(top, TW), pl.ds(left, TW)]

    @pl.loop(0, DOM)
    def _(g):
        @pl.loop(0, FAR)
        def _(i):
            pick(g, i)
            block_copy(g, i).start()

        @pl.loop(1, NEAR)
        def _(v):
            pick(g, FAR + v)
            near_copy(g, v).start()

        pick(g, FAR)
        self_copy(g).start()

    def fill(j, at, base, read):
        cols = pl.ds(pl.multiple_of(j * TW, TW), TW)
        for m in range(2):
            keep = rec_s[at, LANE_ON] * jnp.where(rec_s[at, LANE_ROW] == m, 1, 0)
            scale = keep.astype(jnp.float32)
            for p in range(2):
                part = read(at, p).astype(jnp.float32) * scale
                lhs[pl.ds(base + (2 * m + p) * TW, TW), cols] = part.astype(jnp.bfloat16)

    def mine_at(at, p):
        return ints[p, slot_of(at)]

    @pl.loop(0, HALF)
    def _(j):
        fill(j, half_holder(y0, j), 0, mine_at)

    @pl.loop(0, NEAR)
    def _(v):
        fill(HALF + v, near_holder(v), 0, mine_at)

    rec_doms = [dom_copy(0), dom_copy(1)]
    for copy in rec_doms:
        copy.wait()
    dom_local = pltpu.make_async_copy(domv, dom_s, load_sem.at[4])
    dom_local.start()
    dom_local.wait()

    @pl.loop(0, 8)
    def _(t):
        m, k = lax.div(t, 4), lax.rem(t, 4)
        n = jnp.clip(pair[m, k] - 2 * bas + 2, 0, 5)
        side, row = n >> 1, n & 1
        match_s[t, 12] = side
        match_s[t, 13] = row
        for d in range(DOM):
            at, some = 0, 0
            for e in range(DOM):
                same = jnp.where(dom_s[side, 0, row * DOM + e] == dom[m, d], 1, 0)
                at, some = at + same * e, some + same
            match_s[t, d] = jnp.minimum(at, DOM - 1)
            match_s[t, DOM + d] = some

    def whole(ref, sem):
        return pltpu.make_async_copy(ref, ref, sem)

    def part_copy(g, m):
        return pltpu.make_async_remote_copy(
            src_ref=other.at[g, m], dst_ref=other_in.at[g, m],
            send_sem=part_send.at[g, m], recv_sem=part_recv.at[g, m],
            device_id={"aux": partner}, device_id_type=MESH,
        )

    def halo_copy(g, m, way):
        return pltpu.make_async_remote_copy(
            src_ref=halo.at[1, g, m], dst_ref=halo.at[2 - 2 * way, g, m],
            send_sem=halo_send.at[g, m, way], recv_sem=halo_recv.at[g, m, way],
            device_id={"bas": after if way else before}, device_id_type=MESH,
        )

    def contract_own(g):
        for m in range(2):
            own[g, m] = jnp.dot(
                lhs[2 * m * TW : 2 * (m + 1) * TW, :], rhs[g], preferred_element_type=jnp.float32
            )

    def contract_other(g):
        for m in range(2):
            rows = pl.ds(ROWS + 2 * m * TW, 2 * TW)
            other[g, m] = jnp.dot(
                lhs[rows, : HALF * TW], rhs[g, : HALF * TW, :], preferred_element_type=jnp.float32
            )
            part_copy(g, m).start()

    def finish(g):
        for m in range(2):
            part_copy(g, m).wait_recv()
            for p in range(2):
                rows = pl.ds(p * TW, TW)
                total = own[g, m, rows, :] + other_in[g, m, rows, :]
                halo[1, g, m, :, p * TW : (p + 1) * TW] = total.astype(jnp.bfloat16)
            halo_copy(g, m, 0).start()
            halo_copy(g, m, 1).start()

    def arrived(g):
        self_copy(g).wait()

        @pl.loop(1, NEAR)
        def _(v):
            near_copy(g, v).wait_recv()

        whole(rhs.at[g, pl.ds(FAR * TW, FAR * TW), :], pass_recv.at[g]).wait()

    def hand_on(g, low, high):
        @pl.loop(low, high)
        def _(i):
            block_copy(g, i).wait_recv()
            pass_copy(g, i).start()

    last = DOM - 1
    for g in range(DOM):
        hand_on(g, 0, FAR // 2)
        if g == 3:
            ints_copy.wait_recv()

            @pl.loop(0, HALF)
            def _(j):
                fill(j, half_holder(y0, j), ROWS, lambda at, p: ints_in[j, p])

            contract_other(0)
            contract_other(1)
        if g >= 1:
            arrived(g - 1)
            if g >= 3:
                contract_other(g - 1)
            contract_own(g - 1)
        hand_on(g, FAR // 2, FAR)
        if g == last:
            for early in range(last - 2):
                finish(early)
    arrived(last)
    contract_other(last)
    finish(last - 2)
    contract_own(last)
    finish(last - 1)
    finish(last)
    for g in range(DOM):
        for m in range(2):
            halo_copy(g, m, 0).wait_recv()
            halo_copy(g, m, 1).wait_recv()

    def tile_copy(r):
        owner = lax.rem(y + r, 4)
        return pltpu.make_async_remote_copy(
            src_ref=tiles.at[pl.ds(2 * owner, 2)], dst_ref=tiles_in.at[r - 1],
            send_sem=tile_send.at[r - 1], recv_sem=tile_recv.at[r - 1],
            device_id={"aux": owner}, device_id_type=MESH,
        )

    def res_copy(r):
        return pltpu.make_async_remote_copy(
            src_ref=result.at[pl.ds(2 * y, 2)], dst_ref=result.at[pl.ds(2 * y, 2)],
            send_sem=res_send.at[r - 1], recv_sem=res_recv.at[r - 1],
            device_id={"aux": lax.rem(y + r, 4)}, device_id_type=MESH,
        )

    for r in (2, 1, 3, 0):
        @pl.loop(0, 2)
        def _(s):
            t = 2 * lax.rem(y + r, 4) + s
            side, row = match_s[t, 12], match_s[t, 13]
            total = jnp.zeros((TW, TW), jnp.float32)
            for d in range(DOM):
                there = halo[side, match_s[t, d], row]
                scale = match_s[t, DOM + d].astype(jnp.float32)
                here = halo[1, d, lax.div(t, 4)]
                part = lax.dot_general(
                    here, there, (((1,), (1,)), ((), ())), preferred_element_type=jnp.float32
                )
                total += part * scale
            tiles[t] = total

        if r:
            tile_copy(r).start()
    for r in range(1, 4):
        tile_copy(r).wait_recv()
    total = tiles[pl.ds(2 * y, 2)] + tiles_in[0] + tiles_in[1] + tiles_in[2]
    result[pl.ds(2 * y, 2)] = total.astype(jnp.bfloat16)
    for r in (2, 1, 3):
        res_copy(r).start()

    @pl.loop(0, DOM)
    def _(g):
        @pl.loop(0, FAR)
        def _(i):
            block_copy(g, i).wait_send()

        @pl.loop(1, NEAR)
        def _(v):
            near_copy(g, v).wait_send()

        whole(rhs.at[g, pl.ds(0, FAR * TW), :], pass_send.at[g]).wait()
        for m in range(2):
            part_copy(g, m).wait_send()
            halo_copy(g, m, 0).wait_send()
            halo_copy(g, m, 1).wait_send()

    @pl.loop(0, FAR)
    def _(i):
        rec_far(i).wait_send()

    @pl.loop(1, NEAR)
    def _(v):
        rec_near(v).wait_send()

    ints_copy.wait_send()
    for r in range(1, 4):
        tile_copy(r).wait_send()
        res_copy(r).wait()
    out_ref[...] = result[...]


def on_device(integrals, orbitals, screen_list, screen_count, domains, pair_list):
    vmem = pl.BlockSpec(memory_space=pltpu.VMEM)
    hbm = pl.BlockSpec(memory_space=pltpu.HBM)
    dma, bf16, f32, i32 = pltpu.SemaphoreType.DMA, jnp.bfloat16, jnp.float32, jnp.int32
    out = pl.pallas_call(
        kernel,
        out_shape=jax.ShapeDtypeStruct((8, TW, TW), bf16),
        in_specs=[hbm] * 6,
        out_specs=vmem,
        scratch_shapes=[
            pltpu.VMEM(screen_list.shape, i32),
            pltpu.SMEM(screen_count.shape, i32),
            pltpu.SMEM(domains.shape, i32),
            pltpu.SMEM(pair_list.shape, i32),
            pltpu.VMEM((2, 64, TW, TW), bf16),
            pltpu.VMEM(orbitals.shape, bf16),
            pltpu.VMEM((64, TW), i32),
            pltpu.SMEM((64, TW), i32),
            pltpu.VMEM((24, TW), i32),
            pltpu.SMEM((24, TW), i32),
            pltpu.VMEM((3, 8, TW), i32),
            pltpu.SMEM((3, 8, TW), i32),
            pltpu.SMEM((8, 16), i32),
            pltpu.VMEM((DOM, FAR + NEAR, TW, TW), bf16),
            pltpu.VMEM((DOM, HELD * TW, TW), bf16),
            pltpu.VMEM((HALF, 2, TW, TW), bf16),
            pltpu.VMEM((HALF, 2, TW, TW), bf16),
            pltpu.VMEM((2 * ROWS, HELD * TW), bf16),
            pltpu.VMEM((DOM, 2, 2 * TW, TW), f32),
            pltpu.VMEM((DOM, 2, 2 * TW, TW), f32),
            pltpu.VMEM((DOM, 2, 2 * TW, TW), f32),
            pltpu.VMEM((3, DOM, 2, TW, 2 * TW), bf16),
            pltpu.VMEM((8, TW, TW), f32),
            pltpu.VMEM((3, 2, TW, TW), f32),
            pltpu.VMEM((8, TW, TW), bf16),
            dma((9,)), dma((FAR + NEAR,)), dma((FAR + NEAR,)), dma((2,)), dma((2,)),
            dma((DOM, FAR + NEAR)), dma((DOM, FAR + NEAR)), dma((DOM,)), dma((DOM,)), dma((2,)),
            dma((DOM, 2)), dma((DOM, 2)), dma((DOM, 2, 2)), dma((DOM, 2, 2)),
            dma((3,)), dma((3,)), dma((3,)), dma((3,)),
        ],
        compiler_params=pltpu.CompilerParams(
            collective_id=0, has_side_effects=True, vmem_limit_bytes=64 * 2**20 - 2**16
        ),
    )(
        screen_list, screen_count, domains, pair_list,
        integrals.reshape(2, 64, TW, TW), orbitals,
    )
    return out.reshape(2, 4, TW, TW)


def solution(mesh):
    in_specs = (
        P("aux", "bas", None, None, None),
        P("bas", None),
        P("bas", None),
        P("bas"),
        P("bas", None),
        P("bas", None),
    )
    return jax.shard_map(
        on_device, mesh=mesh, in_specs=in_specs, out_specs=P("bas", None, None, None), check_vma=False
    )
```

```python
import functools

import jax
import jax.numpy as jnp
from jax import lax
from jax.experimental import pallas as pl
from jax.experimental.pallas import tpu as pltpu
from jax.sharding import PartitionSpec as P

MESH = pl.DeviceIdType.MESH
TW = 128
DOM = 6
FAR = 14
NEAR = 8
HALF = 2 * FAR
HELD = HALF + NEAR
AHEAD = 2
ROWS = 4 * TW
LAST = DOM - 1
SIDE, ROW, BACK, SOME_BACK, BOTH = 12, 13, 14, 15, 16
LANE_TILE, LANE_DOM, LANE_SLOT, LANE_ROW, LANE_ON = 0, 1, 7, 8, 9


def kernel(
    lists_ref, count_ref, dom_ref, pair_ref, integrals_ref, orbitals_ref, out_ref,
    lists, count, dom, pair,
    ints, orbs, rec, rec_s, req, req_s, domv, dom_s, match_s,
    sent, rhs, ints_out, ints_in, lhs, own, other, other_in, halo, final, tiles, tiles_in, result,
    load_sem, rec_send, rec_recv, dom_send, dom_recv,
    block_send, block_recv, pass_send, pass_recv, ints_sem,
    part_send, part_recv, halo_send, halo_recv, tile_send, tile_recv, res_send, res_recv,
):
    y, bas = lax.axis_index("aux"), lax.axis_index("bas")
    x, z, c = lax.div(bas, 16), lax.rem(lax.div(bas, 2), 8), lax.rem(bas, 2)
    y0, y1 = lax.rem(y, 2), lax.div(y, 2)
    partner, mate = y + 1 - 2 * y0, 3 - y
    before, after = lax.rem(bas + 63, 64), lax.rem(bas + 1, 64)

    def place(px, pz, pc):
        return lax.rem(px, 4) * 16 + lax.rem(pz, 8) * 2 + pc

    def offset(parity, i):
        v = lax.rem(i, 7)
        dz = 4 + lax.div(v + 1, 2) * (1 - 2 * lax.rem(v, 2))
        return 2 * lax.div(i, 7) + lax.rem(dz + parity, 2), dz

    out_parity = lax.rem(c + y0, 2)
    out_core = lax.rem(y0 + y1 + c, 2)

    def target(i):
        dx, dz = offset(out_parity, i)
        return place(x + 4 - dx, z + 8 - dz, out_core)

    def holder(plane0, plane1, i):
        dx, dz = offset(lax.rem(c + plane1, 2), i)
        return place(x + dx, z + dz, lax.rem(plane0 + plane1 + c, 2))

    def half_holder(plane0, j):
        q = lax.div(j, FAR)
        return holder(lax.rem(plane0 + q, 2), lax.rem(y1 + q, 2), lax.rem(j, FAR))

    def near_target(v):
        return place(x + 4 - lax.div(v, 2), z, lax.rem(c + v, 2))

    def near_holder(v):
        return place(x + lax.div(v, 2), z, lax.rem(c + v, 2))

    small = [
        pltpu.make_async_copy(a, b, load_sem.at[5 + i])
        for i, (a, b) in enumerate(
            [(lists_ref, lists), (count_ref, count), (dom_ref, dom), (pair_ref, pair)]
        )
    ]
    load_ints = pltpu.make_async_copy(integrals_ref, ints, load_sem.at[0])
    load_orbs = pltpu.make_async_copy(orbitals_ref, orbs, load_sem.at[1])
    for copy in small:
        copy.start()
    load_ints.start()
    load_orbs.start()

    barrier = pltpu.get_barrier_semaphore()

    def greet(device):
        pl.semaphore_signal(barrier, inc=1, device_id=device, device_id_type=MESH)

    @pl.loop(0, FAR)
    def _(i):
        greet({"bas": target(i)})
        greet({"bas": holder(y0, y1, i)})

    @pl.loop(1, NEAR)
    def _(v):
        greet({"bas": near_target(v)})

    for r in range(1, 4):
        greet({"aux": lax.rem(y + r, 4)})
    greet({"bas": before})
    greet({"bas": after})

    for copy in small:
        copy.wait()

    holder_ids = lax.broadcasted_iota(jnp.int32, (64, 32), 0)
    slot_ids = lax.broadcasted_iota(jnp.int32, (64, 32), 1)
    lanes = lax.broadcasted_iota(jnp.int32, (64, TW), 1)
    table = jnp.zeros((64, TW), jnp.int32)
    for m in range(2):
        row = lists[m : m + 1, :]
        hit = (row >> 1) == holder_ids
        found = jnp.sum(jnp.where(hit, 1, 0), axis=1, keepdims=True)
        tile = jnp.sum(jnp.where(hit, row & 1, 0), axis=1, keepdims=True)
        slot = jnp.sum(jnp.where(hit, slot_ids, 0), axis=1, keepdims=True)
        on = found * jnp.where(slot < count[m], 1, 0)
        table += jnp.where(lanes == LANE_TILE, tile, 0)
        table += jnp.where(lanes == LANE_SLOT, slot + found * (32 * m), 0)
        table += jnp.where(lanes == LANE_ROW, found * m, 0)
        table += jnp.where(lanes == LANE_ON, on, 0)
        for d in range(DOM):
            table += jnp.where(lanes == LANE_DOM + d, found * dom[m, d], 0)
    rec[...] = jnp.clip(table, 0, 79)
    lane = lax.broadcasted_iota(jnp.int32, (8, TW), 1)
    mine = jnp.zeros((8, TW), jnp.int32)
    for m in range(2):
        for d in range(DOM):
            mine += jnp.where(lane == m * DOM + d, dom[m, d], 0)
    domv[1] = mine
    rec_local = pltpu.make_async_copy(rec, rec_s, load_sem.at[2])
    rec_local.start()

    pl.semaphore_wait(barrier, 2 * FAR + NEAR - 1 + 5)

    def rec_copy(i, device):
        return pltpu.make_async_remote_copy(
            src_ref=rec.at[pl.ds(device, 1), :], dst_ref=req.at[pl.ds(i, 1), :],
            send_sem=rec_send.at[i], recv_sem=rec_recv.at[i],
            device_id={"bas": device}, device_id_type=MESH,
        )

    def rec_far(i):
        return rec_copy(i, holder(y0, y1, i))

    def rec_near(v):
        return rec_copy(FAR + v, near_holder(v))

    rec_self = pltpu.make_async_copy(rec.at[pl.ds(bas, 1), :], req.at[pl.ds(FAR, 1), :], rec_recv.at[FAR])

    @pl.loop(0, FAR)
    def _(i):
        rec_far(i).start()

    @pl.loop(1, NEAR)
    def _(v):
        rec_near(v).start()

    rec_self.start()

    def dom_copy(way):
        return pltpu.make_async_remote_copy(
            src_ref=domv.at[1], dst_ref=domv.at[2 - 2 * way],
            send_sem=dom_send.at[way], recv_sem=dom_recv.at[way],
            device_id={"bas": after if way else before}, device_id_type=MESH,
        )

    dom_copy(0).start()
    dom_copy(1).start()

    def slot_of(at):
        return jnp.minimum(rec_s[at, LANE_SLOT], 63)

    rec_local.wait()
    load_ints.wait()

    @pl.loop(0, HALF)
    def _(j):
        slot = slot_of(half_holder(lax.rem(y0 + 1, 2), j))
        for p in range(2):
            ints_out[j, p] = ints[p, slot]

    ints_copy = pltpu.make_async_remote_copy(
        src_ref=ints_out, dst_ref=ints_in, send_sem=ints_sem.at[0], recv_sem=ints_sem.at[1],
        device_id={"aux": partner}, device_id_type=MESH,
    )
    ints_copy.start()

    rec_self.wait()

    @pl.loop(0, FAR)
    def _(i):
        rec_far(i).wait_recv()

    @pl.loop(1, NEAR)
    def _(v):
        rec_near(v).wait_recv()

    req_local = pltpu.make_async_copy(req, req_s, load_sem.at[3])
    req_local.start()
    req_local.wait()
    load_orbs.wait()

    def rows_of(i):
        return pl.ds(pl.multiple_of(i * TW, TW), TW)

    def block_copy(g, i):
        return pltpu.make_async_remote_copy(
            src_ref=sent.at[g, i], dst_ref=rhs.at[g, rows_of(i), :],
            send_sem=block_send.at[g, i], recv_sem=block_recv.at[g, i],
            device_id={"bas": target(i)}, device_id_type=MESH,
        )

    def near_copy(g, v):
        return pltpu.make_async_remote_copy(
            src_ref=sent.at[g, FAR + v], dst_ref=rhs.at[g, rows_of(HALF + v), :],
            send_sem=block_send.at[g, FAR + v], recv_sem=block_recv.at[g, FAR + v],
            device_id={"bas": near_target(v)}, device_id_type=MESH,
        )

    def self_copy(g):
        return pltpu.make_async_copy(
            sent.at[g, FAR], rhs.at[g, pl.ds(HALF * TW, TW), :], block_recv.at[g, FAR]
        )

    def pass_copy(g, i):
        return pltpu.make_async_remote_copy(
            src_ref=rhs.at[g, rows_of(i), :], dst_ref=rhs.at[g, rows_of(FAR + i), :],
            send_sem=pass_send.at[g], recv_sem=pass_recv.at[g],
            device_id={"aux": mate}, device_id_type=MESH,
        )

    def pick(g, i):
        top = jnp.minimum(req_s[i, LANE_TILE], 1) * TW
        left = req_s[i, LANE_DOM + g] * TW
        sent[g, i] = orbs[pl.ds(top, TW), pl.ds(left, TW)]

    def send_far(g, i):
        pick(g, i)
        block_copy(g, i).start()

    def send_near(g):
        @pl.loop(1, NEAR)
        def _(v):
            pick(g, FAR + v)
            near_copy(g, v).start()

        pick(g, FAR)
        self_copy(g).start()

    for g in range(AHEAD):
        @pl.loop(0, FAR)
        def _(i):
            send_far(g, i)

        send_near(g)

    def fill(j, at, base, read):
        cols = pl.ds(pl.multiple_of(j * TW, TW), TW)
        for m in range(2):
            keep = rec_s[at, LANE_ON] * jnp.where(rec_s[at, LANE_ROW] == m, 1, 0)
            scale = keep.astype(jnp.float32)
            for p in range(2):
                part = read(at, p).astype(jnp.float32) * scale
                lhs[pl.ds(base + (2 * m + p) * TW, TW), cols] = part.astype(jnp.bfloat16)

    def mine_at(at, p):
        return ints[p, slot_of(at)]

    def fill_own():
        @pl.loop(0, HALF)
        def _(j):
            fill(j, half_holder(y0, j), 0, mine_at)

        @pl.loop(0, NEAR)
        def _(v):
            fill(HALF + v, near_holder(v), 0, mine_at)

    def match():
        for way in range(2):
            dom_copy(way).wait()
        dom_local = pltpu.make_async_copy(domv, dom_s, load_sem.at[4])
        dom_local.start()
        dom_local.wait()

        @pl.loop(0, 8)
        def _(t):
            m, k = lax.div(t, 4), lax.rem(t, 4)
            n = jnp.clip(pair[m, k] - 2 * bas + 2, 0, 5)
            side, row = n >> 1, n & 1
            match_s[t, SIDE] = side
            match_s[t, ROW] = row
            back, some_back = 0, 0
            for d in range(DOM):
                at, some = 0, 0
                for e in range(LAST):
                    same = jnp.where(dom_s[side, 0, row * DOM + e] == dom[m, d], 1, 0)
                    at, some = at + same * e, some + same
                match_s[t, d] = jnp.minimum(at, LAST - 1)
                match_s[t, DOM + d] = some
                same = jnp.where(dom_s[side, 0, row * DOM + LAST] == dom[m, d], 1, 0)
                if d < LAST:
                    back, some_back = back + same * d, some_back + same
                else:
                    match_s[t, BOTH] = same
            match_s[t, BACK] = jnp.minimum(back, LAST - 1)
            match_s[t, SOME_BACK] = some_back

    def whole(ref, sem):
        return pltpu.make_async_copy(ref, ref, sem)

    def part_copy(g, m):
        return pltpu.make_async_remote_copy(
            src_ref=other.at[g, m], dst_ref=other_in.at[g, m],
            send_sem=part_send.at[g, m], recv_sem=part_recv.at[g, m],
            device_id={"aux": partner}, device_id_type=MESH,
        )

    def halo_copy(g, m, way):
        return pltpu.make_async_remote_copy(
            src_ref=halo.at[1, g, m] if g < LAST else final.at[1, m],
            dst_ref=halo.at[2 - 2 * way, g, m] if g < LAST else final.at[2 - 2 * way, m],
            send_sem=halo_send.at[g, m, way], recv_sem=halo_recv.at[g, m, way],
            device_id={"bas": after if way else before}, device_id_type=MESH,
        )

    def contract_own(g):
        for m in range(2):
            own[g, m] = jnp.dot(
                lhs[2 * m * TW : 2 * (m + 1) * TW, :], rhs[g], preferred_element_type=jnp.float32
            )

    def contract_other(g):
        for m in range(2):
            rows = pl.ds(ROWS + 2 * m * TW, 2 * TW)
            other[g, m] = jnp.dot(
                lhs[rows, : HALF * TW], rhs[g, : HALF * TW, :], preferred_element_type=jnp.float32
            )
            part_copy(g, m).start()

    def finish(g):
        for m in range(2):
            part_copy(g, m).wait_recv()
            for p in range(2):
                rows = pl.ds(p * TW, TW)
                total = own[g, m, rows, :] + other_in[g, m, rows, :]
                if g < LAST:
                    halo[1, g, m, :, p * TW : (p + 1) * TW] = total.astype(jnp.bfloat16)
                else:
                    final[1, m, :, p * TW : (p + 1) * TW] = total.astype(jnp.bfloat16)
            halo_copy(g, m, 0).start()
            halo_copy(g, m, 1).start()

    def arrived(g):
        self_copy(g).wait()

        @pl.loop(1, NEAR)
        def _(v):
            near_copy(g, v).wait_recv()

        whole(rhs.at[g, pl.ds(FAR * TW, FAR * TW), :], pass_recv.at[g]).wait()

    def hand_on(g, low, high):
        @pl.loop(low, high)
        def _(i):
            if g + AHEAD < DOM:
                send_far(g + AHEAD, i)
            block_copy(g, i).wait_recv()
            pass_copy(g, i).start()

    for g in range(DOM):
        hand_on(g, 0, FAR // 2)
        if g == 0:
            fill_own()
        if g == 3:
            ints_copy.wait_recv()

            @pl.loop(0, HALF)
            def _(j):
                fill(j, half_holder(y0, j), ROWS, lambda at, p: ints_in[j, p])

            contract_other(0)
            contract_other(1)
        if g >= 1:
            arrived(g - 1)
            if g >= 3:
                contract_other(g - 1)
            contract_own(g - 1)
        hand_on(g, FAR // 2, FAR)
        if g + AHEAD < DOM:
            send_near(g + AHEAD)
        if g == 1:
            match()
    def columns(base, m, low, high):
        return jnp.dot(
            lhs[base + 2 * m * TW : base + 2 * (m + 1) * TW, low * TW : high * TW],
            rhs[LAST, low * TW : high * TW, :], preferred_element_type=jnp.float32,
        )

    for m in range(2):
        other[LAST, m] = columns(ROWS, m, 0, FAR)
    for g in range(LAST - 1):
        finish(g)
    for m in range(2):
        own[LAST, m] = columns(0, m, 0, FAR)
    arrived(LAST)
    for m in range(2):
        other[LAST, m] += columns(ROWS, m, FAR, HALF)
        part_copy(LAST, m).start()
    for m in range(2):
        own[LAST, m] += columns(0, m, FAR, HELD)
    finish(LAST - 1)

    def dot(here, there):
        return lax.dot_general(here, there, (((1,), (1,)), ((), ())), preferred_element_type=jnp.float32)

    def flag(t, column):
        return match_s[t, column].astype(jnp.float32)

    def wait_halo(g):
        for m in range(2):
            halo_copy(g, m, 0).wait_recv()
            halo_copy(g, m, 1).wait_recv()

    def pairs(t, domains):
        total = jnp.zeros((TW, TW), jnp.float32)
        for d in domains:
            here = halo[1, d, lax.div(t, 4)] if d < LAST else final[1, lax.div(t, 4)]
            there = halo[match_s[t, SIDE], match_s[t, d], match_s[t, ROW]]
            total += dot(here, there) * flag(t, DOM + d)
        return total

    finish(LAST)
    for g in range(LAST):
        wait_halo(g)

    @pl.loop(0, 8)
    def _(t):
        tiles[t] = pairs(t, range(DOM))

    wait_halo(LAST)

    def tile_copy(r):
        owner = lax.rem(y + r, 4)
        return pltpu.make_async_remote_copy(
            src_ref=tiles.at[pl.ds(2 * owner, 2)], dst_ref=tiles_in.at[r - 1],
            send_sem=tile_send.at[r - 1], recv_sem=tile_recv.at[r - 1],
            device_id={"aux": owner}, device_id_type=MESH,
        )

    def res_copy(r):
        return pltpu.make_async_remote_copy(
            src_ref=result.at[pl.ds(2 * y, 2)], dst_ref=result.at[pl.ds(2 * y, 2)],
            send_sem=res_send.at[r - 1], recv_sem=res_recv.at[r - 1],
            device_id={"aux": lax.rem(y + r, 4)}, device_id_type=MESH,
        )

    for r in (2, 1, 3, 0):
        for s in range(2):
            t = 2 * lax.rem(y + r, 4) + s
            m = lax.div(t, 4)
            here = halo[1, match_s[t, BACK], m].astype(jnp.float32) * flag(t, SOME_BACK)
            here += final[1, m].astype(jnp.float32) * flag(t, BOTH)
            tiles[t] += dot(here.astype(jnp.bfloat16), final[match_s[t, SIDE], match_s[t, ROW]])
        if r:
            tile_copy(r).start()
    for r in range(1, 4):
        tile_copy(r).wait_recv()
    total = tiles[pl.ds(2 * y, 2)] + tiles_in[0] + tiles_in[1] + tiles_in[2]
    result[pl.ds(2 * y, 2)] = total.astype(jnp.bfloat16)
    for r in (2, 1, 3):
        res_copy(r).start()

    @pl.loop(0, DOM)
    def _(g):
        @pl.loop(0, FAR)
        def _(i):
            block_copy(g, i).wait_send()

        @pl.loop(1, NEAR)
        def _(v):
            near_copy(g, v).wait_send()

        whole(rhs.at[g, pl.ds(0, FAR * TW), :], pass_send.at[g]).wait()
        for m in range(2):
            part_copy(g, m).wait_send()

    for g in range(DOM):
        for m in range(2):
            halo_copy(g, m, 0).wait_send()
            halo_copy(g, m, 1).wait_send()

    @pl.loop(0, FAR)
    def _(i):
        rec_far(i).wait_send()

    @pl.loop(1, NEAR)
    def _(v):
        rec_near(v).wait_send()

    ints_copy.wait_send()
    for r in range(1, 4):
        tile_copy(r).wait_send()
        res_copy(r).wait()
    out_ref[...] = result[...]


def on_device(integrals, orbitals, screen_list, screen_count, domains, pair_list):
    vmem = pl.BlockSpec(memory_space=pltpu.VMEM)
    hbm = pl.BlockSpec(memory_space=pltpu.HBM)
    dma, bf16, f32, i32 = pltpu.SemaphoreType.DMA, jnp.bfloat16, jnp.float32, jnp.int32
    out = pl.pallas_call(
        kernel,
        out_shape=jax.ShapeDtypeStruct((8, TW, TW), bf16),
        in_specs=[hbm] * 6,
        out_specs=vmem,
        scratch_shapes=[
            pltpu.VMEM(screen_list.shape, i32),
            pltpu.SMEM(screen_count.shape, i32),
            pltpu.SMEM(domains.shape, i32),
            pltpu.SMEM(pair_list.shape, i32),
            pltpu.VMEM((2, 64, TW, TW), bf16),
            pltpu.VMEM(orbitals.shape, bf16),
            pltpu.VMEM((64, TW), i32),
            pltpu.SMEM((64, TW), i32),
            pltpu.VMEM((24, TW), i32),
            pltpu.SMEM((24, TW), i32),
            pltpu.VMEM((3, 8, TW), i32),
            pltpu.SMEM((3, 8, TW), i32),
            pltpu.SMEM((8, 24), i32),
            pltpu.VMEM((DOM, FAR + NEAR, TW, TW), bf16),
            pltpu.VMEM((DOM, HELD * TW, TW), bf16),
            pltpu.VMEM((HALF, 2, TW, TW), bf16),
            pltpu.VMEM((HALF, 2, TW, TW), bf16),
            pltpu.VMEM((2 * ROWS, HELD * TW), bf16),
            pltpu.VMEM((DOM, 2, 2 * TW, TW), f32),
            pltpu.VMEM((DOM, 2, 2 * TW, TW), f32),
            pltpu.VMEM((DOM, 2, 2 * TW, TW), f32),
            pltpu.VMEM((3, LAST, 2, TW, 2 * TW), bf16),
            pltpu.VMEM((3, 2, TW, 2 * TW), bf16),
            pltpu.VMEM((8, TW, TW), f32),
            pltpu.VMEM((3, 2, TW, TW), f32),
            pltpu.VMEM((8, TW, TW), bf16),
            dma((9,)), dma((FAR + NEAR,)), dma((FAR + NEAR,)), dma((2,)), dma((2,)),
            dma((DOM, FAR + NEAR)), dma((DOM, FAR + NEAR)), dma((DOM,)), dma((DOM,)), dma((2,)),
            dma((DOM, 2)), dma((DOM, 2)), dma((DOM, 2, 2)), dma((DOM, 2, 2)),
            dma((3,)), dma((3,)), dma((3,)), dma((3,)),
        ],
        compiler_params=pltpu.CompilerParams(
            collective_id=0, has_side_effects=True, vmem_limit_bytes=64 * 2**20 - 2**16
        ),
    )(
        screen_list, screen_count, domains, pair_list,
        integrals.reshape(2, 64, TW, TW), orbitals,
    )
    return out.reshape(2, 4, TW, TW)


def solution(mesh):
    in_specs = (
        P("aux", "bas", None, None, None),
        P("bas", None),
        P("bas", None),
        P("bas"),
        P("bas", None),
        P("bas", None),
    )
    return jax.shard_map(
        on_device, mesh=mesh, in_specs=in_specs, out_specs=P("bas", None, None, None), check_vma=False
    )
```

```python
import functools

import jax
import jax.numpy as jnp
from jax import lax
from jax.experimental import pallas as pl
from jax.experimental.pallas import tpu as pltpu
from jax.sharding import PartitionSpec as P

MESH = pl.DeviceIdType.MESH
TW = 128
DOM = 6
FAR = 14
NEAR = 8
HALF = 2 * FAR
HELD = HALF + NEAR
AHEAD = 2
ROWS = 4 * TW
LAST = DOM - 1
SIDE, ROW, BACK, SOME_BACK, BOTH = 12, 13, 14, 15, 16
LANE_TILE, LANE_DOM, LANE_SLOT, LANE_ROW, LANE_ON = 0, 1, 7, 8, 9


def kernel(
    lists_ref, count_ref, dom_ref, pair_ref, integrals_ref, orbitals_ref, out_ref,
    lists, count, dom, pair,
    ints, orbs, rec, rec_s, req, req_s, domv, dom_s, match_s,
    sent, rhs, ints_out, ints_in, lhs, own, other, other_in, halo, final, tiles, tiles_in, result,
    load_sem, rec_send, rec_recv, dom_send, dom_recv,
    block_send, block_recv, pass_send, pass_recv, ints_sem,
    part_send, part_recv, halo_send, halo_recv, tile_send, tile_recv, res_send, res_recv,
):
    y, bas = lax.axis_index("aux"), lax.axis_index("bas")
    x, z, c = lax.div(bas, 16), lax.rem(lax.div(bas, 2), 8), lax.rem(bas, 2)
    y0, y1 = lax.rem(y, 2), lax.div(y, 2)
    partner, mate = y + 1 - 2 * y0, 3 - y
    before, after = lax.rem(bas + 63, 64), lax.rem(bas + 1, 64)

    def place(px, pz, pc):
        return lax.rem(px, 4) * 16 + lax.rem(pz, 8) * 2 + pc

    def offset(parity, i):
        v = lax.rem(i, 7)
        dz = 4 + lax.div(v + 1, 2) * (1 - 2 * lax.rem(v, 2))
        return 2 * lax.div(i, 7) + lax.rem(dz + parity, 2), dz

    out_parity = lax.rem(c + y0, 2)
    out_core = lax.rem(y0 + y1 + c, 2)

    def target(i):
        dx, dz = offset(out_parity, i)
        return place(x + 4 - dx, z + 8 - dz, out_core)

    def holder(plane0, plane1, i):
        dx, dz = offset(lax.rem(c + plane1, 2), i)
        return place(x + dx, z + dz, lax.rem(plane0 + plane1 + c, 2))

    def half_holder(plane0, j):
        q = lax.div(j, FAR)
        return holder(lax.rem(plane0 + q, 2), lax.rem(y1 + q, 2), lax.rem(j, FAR))

    def near_target(v):
        return place(x + 4 - lax.div(v, 2), z, lax.rem(c + v, 2))

    def near_holder(v):
        return place(x + lax.div(v, 2), z, lax.rem(c + v, 2))

    small = [
        pltpu.make_async_copy(a, b, load_sem.at[5 + i])
        for i, (a, b) in enumerate(
            [(lists_ref, lists), (count_ref, count), (dom_ref, dom), (pair_ref, pair)]
        )
    ]
    load_ints = pltpu.make_async_copy(integrals_ref, ints, load_sem.at[0])
    load_orbs = pltpu.make_async_copy(orbitals_ref, orbs, load_sem.at[1])
    for copy in small:
        copy.start()
    load_ints.start()
    load_orbs.start()

    barrier = pltpu.get_barrier_semaphore()

    def greet(device):
        pl.semaphore_signal(barrier, inc=1, device_id=device, device_id_type=MESH)

    @pl.loop(0, FAR)
    def _(i):
        greet({"bas": target(i)})
        greet({"bas": holder(y0, y1, i)})

    @pl.loop(1, NEAR)
    def _(v):
        greet({"bas": near_target(v)})

    for r in range(1, 4):
        greet({"aux": lax.rem(y + r, 4)})
    greet({"bas": before})
    greet({"bas": after})

    for copy in small:
        copy.wait()

    holder_ids = lax.broadcasted_iota(jnp.int32, (64, 32), 0)
    slot_ids = lax.broadcasted_iota(jnp.int32, (64, 32), 1)
    lanes = lax.broadcasted_iota(jnp.int32, (64, TW), 1)
    table = jnp.zeros((64, TW), jnp.int32)
    for m in range(2):
        row = lists[m : m + 1, :]
        hit = (row >> 1) == holder_ids
        found = jnp.sum(jnp.where(hit, 1, 0), axis=1, keepdims=True)
        tile = jnp.sum(jnp.where(hit, row & 1, 0), axis=1, keepdims=True)
        slot = jnp.sum(jnp.where(hit, slot_ids, 0), axis=1, keepdims=True)
        on = found * jnp.where(slot < count[m], 1, 0)
        table += jnp.where(lanes == LANE_TILE, tile, 0)
        table += jnp.where(lanes == LANE_SLOT, slot + found * (32 * m), 0)
        table += jnp.where(lanes == LANE_ROW, found * m, 0)
        table += jnp.where(lanes == LANE_ON, on, 0)
        for d in range(DOM):
            table += jnp.where(lanes == LANE_DOM + d, found * dom[m, d], 0)
    rec[...] = jnp.clip(table, 0, 79)
    lane = lax.broadcasted_iota(jnp.int32, (8, TW), 1)
    mine = jnp.zeros((8, TW), jnp.int32)
    for m in range(2):
        for d in range(DOM):
            mine += jnp.where(lane == m * DOM + d, dom[m, d], 0)
    domv[1] = mine
    rec_local = pltpu.make_async_copy(rec, rec_s, load_sem.at[2])
    rec_local.start()

    pl.semaphore_wait(barrier, 2 * FAR + NEAR - 1 + 5)

    def rec_copy(i, device):
        return pltpu.make_async_remote_copy(
            src_ref=rec.at[pl.ds(device, 1), :], dst_ref=req.at[pl.ds(i, 1), :],
            send_sem=rec_send.at[i], recv_sem=rec_recv.at[i],
            device_id={"bas": device}, device_id_type=MESH,
        )

    def rec_far(i):
        return rec_copy(i, holder(y0, y1, i))

    def rec_near(v):
        return rec_copy(FAR + v, near_holder(v))

    rec_self = pltpu.make_async_copy(rec.at[pl.ds(bas, 1), :], req.at[pl.ds(FAR, 1), :], rec_recv.at[FAR])

    @pl.loop(0, FAR)
    def _(i):
        rec_far(i).start()

    @pl.loop(1, NEAR)
    def _(v):
        rec_near(v).start()

    rec_self.start()

    def dom_copy(way):
        return pltpu.make_async_remote_copy(
            src_ref=domv.at[1], dst_ref=domv.at[2 - 2 * way],
            send_sem=dom_send.at[way], recv_sem=dom_recv.at[way],
            device_id={"bas": after if way else before}, device_id_type=MESH,
        )

    dom_copy(0).start()
    dom_copy(1).start()

    def slot_of(at):
        return jnp.minimum(rec_s[at, LANE_SLOT], 63)

    rec_local.wait()
    load_ints.wait()

    @pl.loop(0, HALF)
    def _(j):
        slot = slot_of(half_holder(lax.rem(y0 + 1, 2), j))
        for p in range(2):
            ints_out[j, p] = ints[p, slot]

    ints_copy = pltpu.make_async_remote_copy(
        src_ref=ints_out, dst_ref=ints_in, send_sem=ints_sem.at[0], recv_sem=ints_sem.at[1],
        device_id={"aux": partner}, device_id_type=MESH,
    )
    ints_copy.start()

    def to_scalars(low, high):
        rows = pl.ds(low, high - low)
        copy = pltpu.make_async_copy(req.at[rows, :], req_s.at[rows, :], load_sem.at[3])
        copy.start()
        copy.wait()

    load_orbs.wait()

    def rows_of(i):
        return pl.ds(pl.multiple_of(i * TW, TW), TW)

    def block_copy(g, i):
        return pltpu.make_async_remote_copy(
            src_ref=sent.at[g, i], dst_ref=rhs.at[g, rows_of(i), :],
            send_sem=block_send.at[g, i], recv_sem=block_recv.at[g, i],
            device_id={"bas": target(i)}, device_id_type=MESH,
        )

    def near_copy(g, v):
        return pltpu.make_async_remote_copy(
            src_ref=sent.at[g, FAR + v], dst_ref=rhs.at[g, rows_of(HALF + v), :],
            send_sem=block_send.at[g, FAR + v], recv_sem=block_recv.at[g, FAR + v],
            device_id={"bas": near_target(v)}, device_id_type=MESH,
        )

    def self_copy(g):
        return pltpu.make_async_copy(
            sent.at[g, FAR], rhs.at[g, pl.ds(HALF * TW, TW), :], block_recv.at[g, FAR]
        )

    def pass_copy(g, i):
        return pltpu.make_async_remote_copy(
            src_ref=rhs.at[g, rows_of(i), :], dst_ref=rhs.at[g, rows_of(FAR + i), :],
            send_sem=pass_send.at[g], recv_sem=pass_recv.at[g],
            device_id={"aux": mate}, device_id_type=MESH,
        )

    def pick(g, i):
        top = jnp.minimum(req_s[i, LANE_TILE], 1) * TW
        left = req_s[i, LANE_DOM + g] * TW
        sent[g, i] = orbs[pl.ds(top, TW), pl.ds(left, TW)]

    def send_far(g, i):
        pick(g, i)
        block_copy(g, i).start()

    def send_near(g):
        @pl.loop(1, NEAR)
        def _(v):
            pick(g, FAR + v)
            near_copy(g, v).start()

        pick(g, FAR)
        self_copy(g).start()

    for g in range(AHEAD):
        for low, high in ((0, 8), (8, FAR)):
            if g == 0:
                @pl.loop(low, high)
                def _(i):
                    rec_far(i).wait_recv()

                if low:
                    rec_self.wait()

                    @pl.loop(1, NEAR)
                    def _(v):
                        rec_near(v).wait_recv()

                to_scalars(low, 24 if low else high)

            @pl.loop(low, high)
            def _(i):
                send_far(g, i)

        send_near(g)

    def fill(j, at, base, read):
        cols = pl.ds(pl.multiple_of(j * TW, TW), TW)
        for m in range(2):
            keep = rec_s[at, LANE_ON] * jnp.where(rec_s[at, LANE_ROW] == m, 1, 0)
            scale = keep.astype(jnp.float32)
            for p in range(2):
                part = read(at, p).astype(jnp.float32) * scale
                lhs[pl.ds(base + (2 * m + p) * TW, TW), cols] = part.astype(jnp.bfloat16)

    def mine_at(at, p):
        return ints[p, slot_of(at)]

    def fill_own():
        @pl.loop(0, HALF)
        def _(j):
            fill(j, half_holder(y0, j), 0, mine_at)

        @pl.loop(0, NEAR)
        def _(v):
            fill(HALF + v, near_holder(v), 0, mine_at)

    def match():
        for way in range(2):
            dom_copy(way).wait()
        dom_local = pltpu.make_async_copy(domv, dom_s, load_sem.at[4])
        dom_local.start()
        dom_local.wait()

        @pl.loop(0, 8)
        def _(t):
            m, k = lax.div(t, 4), lax.rem(t, 4)
            n = jnp.clip(pair[m, k] - 2 * bas + 2, 0, 5)
            side, row = n >> 1, n & 1
            match_s[t, SIDE] = side
            match_s[t, ROW] = row
            back, some_back = 0, 0
            for d in range(DOM):
                at, some = 0, 0
                for e in range(LAST):
                    same = jnp.where(dom_s[side, 0, row * DOM + e] == dom[m, d], 1, 0)
                    at, some = at + same * e, some + same
                match_s[t, d] = jnp.minimum(at, LAST - 1)
                match_s[t, DOM + d] = some
                same = jnp.where(dom_s[side, 0, row * DOM + LAST] == dom[m, d], 1, 0)
                if d < LAST:
                    back, some_back = back + same * d, some_back + same
                else:
                    match_s[t, BOTH] = same
            match_s[t, BACK] = jnp.minimum(back, LAST - 1)
            match_s[t, SOME_BACK] = some_back

    def whole(ref, sem):
        return pltpu.make_async_copy(ref, ref, sem)

    def part_copy(g, m):
        return pltpu.make_async_remote_copy(
            src_ref=other.at[g, m], dst_ref=other_in.at[g, m],
            send_sem=part_send.at[g, m], recv_sem=part_recv.at[g, m],
            device_id={"aux": partner}, device_id_type=MESH,
        )

    def halo_copy(g, m, way):
        return pltpu.make_async_remote_copy(
            src_ref=halo.at[1, g, m] if g < LAST else final.at[1, m],
            dst_ref=halo.at[2 - 2 * way, g, m] if g < LAST else final.at[2 - 2 * way, m],
            send_sem=halo_send.at[g, m, way], recv_sem=halo_recv.at[g, m, way],
            device_id={"bas": after if way else before}, device_id_type=MESH,
        )

    def contract_own(g):
        for m in range(2):
            own[g, m] = jnp.dot(
                lhs[2 * m * TW : 2 * (m + 1) * TW, :], rhs[g], preferred_element_type=jnp.float32
            )

    def contract_other(g):
        for m in range(2):
            rows = pl.ds(ROWS + 2 * m * TW, 2 * TW)
            other[g, m] = jnp.dot(
                lhs[rows, : HALF * TW], rhs[g, : HALF * TW, :], preferred_element_type=jnp.float32
            )
            part_copy(g, m).start()

    def finish(g):
        for m in range(2):
            part_copy(g, m).wait_recv()
            for p in range(2):
                rows = pl.ds(p * TW, TW)
                total = own[g, m, rows, :] + other_in[g, m, rows, :]
                if g < LAST:
                    halo[1, g, m, :, p * TW : (p + 1) * TW] = total.astype(jnp.bfloat16)
                else:
                    final[1, m, :, p * TW : (p + 1) * TW] = total.astype(jnp.bfloat16)
            halo_copy(g, m, 0).start()
            halo_copy(g, m, 1).start()

    def arrived(g):
        self_copy(g).wait()

        @pl.loop(1, NEAR)
        def _(v):
            near_copy(g, v).wait_recv()

        whole(rhs.at[g, pl.ds(FAR * TW, FAR * TW), :], pass_recv.at[g]).wait()

    def hand_on(g, low, high):
        @pl.loop(low, high)
        def _(i):
            if g + AHEAD < DOM:
                send_far(g + AHEAD, i)
            block_copy(g, i).wait_recv()
            pass_copy(g, i).start()

    for g in range(DOM):
        hand_on(g, 0, FAR // 2)
        if g == 0:
            fill_own()
        if g == 3:
            ints_copy.wait_recv()

            @pl.loop(0, HALF)
            def _(j):
                fill(j, half_holder(y0, j), ROWS, lambda at, p: ints_in[j, p])

            contract_other(0)
            contract_other(1)
        if g >= 1:
            arrived(g - 1)
            if g >= 3:
                contract_other(g - 1)
            contract_own(g - 1)
        hand_on(g, FAR // 2, FAR)
        if g + AHEAD < DOM:
            send_near(g + AHEAD)
        if g == 1:
            match()
    def columns(base, m, low, high):
        return jnp.dot(
            lhs[base + 2 * m * TW : base + 2 * (m + 1) * TW, low * TW : high * TW],
            rhs[LAST, low * TW : high * TW, :], preferred_element_type=jnp.float32,
        )

    for m in range(2):
        other[LAST, m] = columns(ROWS, m, 0, FAR)
    for g in range(LAST - 1):
        finish(g)
    for m in range(2):
        own[LAST, m] = columns(0, m, 0, FAR)
    arrived(LAST)
    for m in range(2):
        other[LAST, m] += columns(ROWS, m, FAR, HALF)
        part_copy(LAST, m).start()
    for m in range(2):
        own[LAST, m] += columns(0, m, FAR, HELD)
    finish(LAST - 1)

    def dot(here, there):
        return lax.dot_general(here, there, (((1,), (1,)), ((), ())), preferred_element_type=jnp.float32)

    def flag(t, column):
        return match_s[t, column].astype(jnp.float32)

    def wait_halo(g):
        for m in range(2):
            halo_copy(g, m, 0).wait_recv()
            halo_copy(g, m, 1).wait_recv()

    def pairs(t, domains):
        total = jnp.zeros((TW, TW), jnp.float32)
        for d in domains:
            here = halo[1, d, lax.div(t, 4)] if d < LAST else final[1, lax.div(t, 4)]
            there = halo[match_s[t, SIDE], match_s[t, d], match_s[t, ROW]]
            total += dot(here, there) * flag(t, DOM + d)
        return total

    finish(LAST)
    for g in range(LAST):
        wait_halo(g)

    @pl.loop(0, 8)
    def _(t):
        tiles[t] = pairs(t, range(DOM))

    wait_halo(LAST)

    def tile_copy(r):
        owner = lax.rem(y + r, 4)
        return pltpu.make_async_remote_copy(
            src_ref=tiles.at[pl.ds(2 * owner, 2)], dst_ref=tiles_in.at[r - 1],
            send_sem=tile_send.at[r - 1], recv_sem=tile_recv.at[r - 1],
            device_id={"aux": owner}, device_id_type=MESH,
        )

    def res_copy(r):
        return pltpu.make_async_remote_copy(
            src_ref=result.at[pl.ds(2 * y, 2)], dst_ref=result.at[pl.ds(2 * y, 2)],
            send_sem=res_send.at[r - 1], recv_sem=res_recv.at[r - 1],
            device_id={"aux": lax.rem(y + r, 4)}, device_id_type=MESH,
        )

    for r in (2, 1, 3, 0):
        for s in range(2):
            t = 2 * lax.rem(y + r, 4) + s
            m = lax.div(t, 4)
            here = halo[1, match_s[t, BACK], m].astype(jnp.float32) * flag(t, SOME_BACK)
            here += final[1, m].astype(jnp.float32) * flag(t, BOTH)
            tiles[t] += dot(here.astype(jnp.bfloat16), final[match_s[t, SIDE], match_s[t, ROW]])
        if r:
            tile_copy(r).start()
    for r in range(1, 4):
        tile_copy(r).wait_recv()
    total = tiles[pl.ds(2 * y, 2)] + tiles_in[0] + tiles_in[1] + tiles_in[2]
    result[pl.ds(2 * y, 2)] = total.astype(jnp.bfloat16)
    for r in (2, 1, 3):
        res_copy(r).start()

    @pl.loop(0, DOM)
    def _(g):
        @pl.loop(0, FAR)
        def _(i):
            block_copy(g, i).wait_send()

        @pl.loop(1, NEAR)
        def _(v):
            near_copy(g, v).wait_send()

        whole(rhs.at[g, pl.ds(0, FAR * TW), :], pass_send.at[g]).wait()
        for m in range(2):
            part_copy(g, m).wait_send()

    for g in range(DOM):
        for m in range(2):
            halo_copy(g, m, 0).wait_send()
            halo_copy(g, m, 1).wait_send()

    @pl.loop(0, FAR)
    def _(i):
        rec_far(i).wait_send()

    @pl.loop(1, NEAR)
    def _(v):
        rec_near(v).wait_send()

    ints_copy.wait_send()
    for r in range(1, 4):
        tile_copy(r).wait_send()
        res_copy(r).wait()
    out_ref[...] = result[...]


def on_device(integrals, orbitals, screen_list, screen_count, domains, pair_list):
    vmem = pl.BlockSpec(memory_space=pltpu.VMEM)
    hbm = pl.BlockSpec(memory_space=pltpu.HBM)
    dma, bf16, f32, i32 = pltpu.SemaphoreType.DMA, jnp.bfloat16, jnp.float32, jnp.int32
    out = pl.pallas_call(
        kernel,
        out_shape=jax.ShapeDtypeStruct((8, TW, TW), bf16),
        in_specs=[hbm] * 6,
        out_specs=vmem,
        scratch_shapes=[
            pltpu.VMEM(screen_list.shape, i32),
            pltpu.SMEM(screen_count.shape, i32),
            pltpu.SMEM(domains.shape, i32),
            pltpu.SMEM(pair_list.shape, i32),
            pltpu.VMEM((2, 64, TW, TW), bf16),
            pltpu.VMEM(orbitals.shape, bf16),
            pltpu.VMEM((64, TW), i32),
            pltpu.SMEM((64, TW), i32),
            pltpu.VMEM((24, TW), i32),
            pltpu.SMEM((24, TW), i32),
            pltpu.VMEM((3, 8, TW), i32),
            pltpu.SMEM((3, 8, TW), i32),
            pltpu.SMEM((8, 24), i32),
            pltpu.VMEM((DOM, FAR + NEAR, TW, TW), bf16),
            pltpu.VMEM((DOM, HELD * TW, TW), bf16),
            pltpu.VMEM((HALF, 2, TW, TW), bf16),
            pltpu.VMEM((HALF, 2, TW, TW), bf16),
            pltpu.VMEM((2 * ROWS, HELD * TW), bf16),
            pltpu.VMEM((DOM, 2, 2 * TW, TW), f32),
            pltpu.VMEM((DOM, 2, 2 * TW, TW), f32),
            pltpu.VMEM((DOM, 2, 2 * TW, TW), f32),
            pltpu.VMEM((3, LAST, 2, TW, 2 * TW), bf16),
            pltpu.VMEM((3, 2, TW, 2 * TW), bf16),
            pltpu.VMEM((8, TW, TW), f32),
            pltpu.VMEM((3, 2, TW, TW), f32),
            pltpu.VMEM((8, TW, TW), bf16),
            dma((9,)), dma((FAR + NEAR,)), dma((FAR + NEAR,)), dma((2,)), dma((2,)),
            dma((DOM, FAR + NEAR)), dma((DOM, FAR + NEAR)), dma((DOM,)), dma((DOM,)), dma((2,)),
            dma((DOM, 2)), dma((DOM, 2)), dma((DOM, 2, 2)), dma((DOM, 2, 2)),
            dma((3,)), dma((3,)), dma((3,)), dma((3,)),
        ],
        compiler_params=pltpu.CompilerParams(
            collective_id=0, has_side_effects=True, vmem_limit_bytes=64 * 2**20 - 2**16
        ),
    )(
        screen_list, screen_count, domains, pair_list,
        integrals.reshape(2, 64, TW, TW), orbitals,
    )
    return out.reshape(2, 4, TW, TW)


def solution(mesh):
    in_specs = (
        P("aux", "bas", None, None, None),
        P("bas", None),
        P("bas", None),
        P("bas"),
        P("bas", None),
        P("bas", None),
    )
    return jax.shard_map(
        on_device, mesh=mesh, in_specs=in_specs, out_specs=P("bas", None, None, None), check_vma=False
    )
```
